256 devices in a mesh: expert: 64 (over z, x, core), tensor: 4 (over y).
Axes of the slice: x: 4, y: 4, z: 8, core: 2. Of those that a mesh axis runs over, the one named last changes fastest.
Arguments:
- tokens: bfloat16 [16384, 1024], P('expert'), may hold values from -6 to 6
- routes: int32 [16384, 2], P('expert'), may hold values from 0 to 63, all different within a row; in each aligned block of 256 rows (0 to 255, 256 to 511, ...) at most 16 rows name the same one
- mix_weights: float32 [16384, 2], P('expert'), may hold values from 0.2 to 1
- w_gate: bfloat16 [64, 1024, 2048], P('expert', None, 'tensor'), may hold values from -0.1875 to 0.1875
- w_up: bfloat16 [64, 1024, 2048], P('expert', None, 'tensor'), may hold values from -0.1875 to 0.1875
- w_down: bfloat16 [64, 2048, 1024], P('expert', 'tensor'), may hold values from -0.125 to 0.125
- cotangent: bfloat16 [16384, 1024], P('expert'), may hold values from -6 to 6
Outputs:
- result: bfloat16 [16384, 1024], P('expert')
- grad_tokens: bfloat16 [16384, 1024], P('expert')
- grad_gate: float32 [64, 1024, 2048], P('expert', None, 'tensor')
- grad_up: float32 [64, 1024, 2048], P('expert', None, 'tensor')
- grad_down: float32 [64, 2048, 1024], P('expert', 'tensor')
The draws below stay inside these ranges and needn't reach their ends.
Inputs may be any that keep to these rules, and one draw needn't show every extreme that they name: `routes`: each row names two different experts. Within each aligned block of 256 rows no expert is named by more than 16 rows, a bound that some block reaches.
All inputs are finite; a program needn't handle non-finite values.
Results may differ from the reference program's by a relative error of at most 0.015.
Values may be sent and summed in bfloat16 or wider, within the bound.
No kernel may reach another device: no remote copies, remote signals or barrier semaphores. Data moves between devices by JAX's collectives and lax.ppermute only.
A program may use at most 128 MiB of HBM per device.

```python
import math
import jax
import jax.numpy as jnp
import numpy as np
from jax import lax

D = 1024
FF = 2048
TOK_DEV = 256
EXPERTS = 64
CAP = 16
TOKENS = 16384
N_EXPERT = 64
N_TENSOR = 4


def block_levels(key, dims, split, low, largest):
    def one(axis_at, blocks):
        draws = jax.random.uniform(jax.random.fold_in(jax.random.fold_in(key, 6), axis_at), (blocks,), jnp.float32, low / len(split), largest / len(split))
        return jnp.repeat(jnp.exp(draws), dims[axis_at] // blocks).reshape((-1,) + (1,) * (len(dims) - axis_at - 1))

    loudness = one(*split[0])
    for cut in split[1:]:
        loudness = loudness * one(*cut)
    return loudness


def routed_block(rng, own, number, rows, count, top, reach, slope):
    ranking = jax.random.permutation(rng, count)
    packed, ordinary = load_shares(count, rows * top, reach, slope, True), load_shares(count, rows * top, reach, slope, False)
    places = jnp.arange(count)

    def named(tallies, offset_by):
        used = int((tallies > 0).sum())
        fixed = max(1, used // 4)
        shifted = fixed + (places - fixed + offset_by * (used - fixed)) % max(1, count - fixed)
        return jnp.zeros((count,), jnp.int32).at[ranking[jnp.where(places < fixed, places, shifted)]].set(jnp.asarray(tallies, jnp.int32))

    tallies = jnp.where(number % 4 == 0, named(packed, number // 4), named(ordinary, number - number // 4 - 1))
    mixed = jax.random.permutation(jax.random.fold_in(own, 3), count)
    giver, taker = mixed[0:count // 2 * 2:2], mixed[1:count // 2 * 2:2]
    room = jnp.minimum(tallies[giver] - 1, reach - tallies[taker]) // 2
    room = jnp.where((giver == ranking[0]) | (taker == ranking[0]) | (tallies[taker] == 0), 0, jnp.maximum(room, 0))
    shifted = jax.random.randint(jax.random.fold_in(own, 4), (count // 2,), 0, 1 << 20) % (room + 1)
    tallies = tallies.at[giver].add(-shifted).at[taker].add(shifted)
    members = jnp.searchsorted(jnp.cumsum(tallies), jnp.arange(rows * top), side="right").astype(jnp.int32)
    listing = members.reshape(top, rows).T
    listing = listing[jax.random.permutation(jax.random.fold_in(own, 1), rows)]
    offset_by = jax.random.randint(jax.random.fold_in(own, 2), (rows, 1), 0, top)
    return jnp.take_along_axis(listing, (jnp.arange(top)[None, :] + offset_by) % top, axis=1)


def load_shares(count, total, bound, slope, full):
    weights = [(1 << 20) // math.isqrt(rank ** slope) + 1 for rank in range(1, count + 1)]
    largest = bound if full else min(bound, max(-(-total // count), total * weights[0] // sum(weights)))
    least = 1 if total - largest >= count - 1 else 0
    counts, rest = [largest] + [least] * (count - 1), total - largest - least * (count - 1)
    while rest > 0:
        movable = [i for i in range(1, count) if counts[i] < largest] or [i for i in range(1, count) if counts[i] < bound]
        pool, left = sum([weights[i] for i in movable]), rest
        for i in movable:
            extra = min(bound - counts[i], max(1, left * weights[i] // pool), rest)
            counts[i] = counts[i] + extra
            rest = rest - extra
    return np.array(counts)


def normal_values(rng, shape, width, most, split=(), kind=jnp.bfloat16):
    entries = jax.random.normal(rng, shape, jnp.float32) * width
    if len(split) > 0:
        entries = block_levels(rng, shape, split, -0.22, 0.18) * entries
    return jnp.clip(entries, min=-most, max=most).astype(kind)


def setup_inputs(seed: int = 0) -> dict:
    splits = jax.random.split(jax.random.key(seed), 8)
    tokens = normal_values(splits[0], (TOKENS, D), 1.0, 6.0, ((0, 64),))
    routes_keys = jax.random.split(jax.random.fold_in(splits[1], 1), TOKENS // TOK_DEV)
    routes_turns = jax.random.permutation(jax.random.fold_in(splits[1], 3), TOKENS // TOK_DEV)
    routes = jax.vmap(lambda own, number: routed_block(jax.random.fold_in(splits[1], 2), own, number, TOK_DEV, EXPERTS, 2, CAP, 2))(routes_keys, routes_turns).reshape((TOKENS, 2))
    mix_weights = jnp.clip(0.2 + 0.8 * jax.random.uniform(splits[2], (TOKENS, 2), jnp.float32) ** block_levels(splits[2], (TOKENS, 2), ((0, 64),), -0.2, 0.2), 0.2, 1.0)
    w_gate = normal_values(splits[3], (EXPERTS, D, FF), D ** -0.5, 0.1875, ((0, 64), (2, 4)))
    w_up = normal_values(splits[4], (EXPERTS, D, FF), D ** -0.5, 0.1875, ((0, 64), (2, 4)))
    w_down = normal_values(splits[5], (EXPERTS, FF, D), FF ** -0.5, 0.125, ((0, 64), (1, 4)))
    cotangent = normal_values(splits[6], (TOKENS, D), 1.0, 6.0, ((0, 64),))
    return {"tokens": tokens, "routes": routes, "mix_weights": mix_weights, "w_gate": w_gate, "w_up": w_up, "w_down": w_down, "cotangent": cotangent}


def expert_forward(received, gate_local, up_local, down_local):
    pre_gate = jnp.dot(received, gate_local, preferred_element_type=jnp.float32)
    pre_up = jnp.dot(received, up_local, preferred_element_type=jnp.float32)
    hidden = (jax.nn.silu(pre_gate) * pre_up).astype(jnp.bfloat16)
    partial_out = jnp.dot(hidden, down_local, preferred_element_type=jnp.float32)
    return pre_gate, pre_up, hidden, partial_out


def expert_backward(received, upstream, pre_gate, pre_up, hidden, gate_local, up_local, down_local):
    contract_last = (((1,), (1,)), ((), ()))
    contract_first = (((0,), (0,)), ((), ()))
    d_hidden = lax.dot_general(upstream, down_local, contract_last, preferred_element_type=jnp.float32)
    sigma = jax.nn.sigmoid(pre_gate)
    d_gate = (d_hidden * pre_up * sigma * (1.0 + pre_gate * (1.0 - sigma))).astype(jnp.bfloat16)
    d_up = (d_hidden * pre_gate * sigma).astype(jnp.bfloat16)
    grad_down = lax.dot_general(hidden, upstream, contract_first, preferred_element_type=jnp.float32)
    grad_gate = lax.dot_general(received, d_gate, contract_first, preferred_element_type=jnp.float32)
    grad_up = lax.dot_general(received, d_up, contract_first, preferred_element_type=jnp.float32)
    partial_in = lax.dot_general(d_gate, gate_local, contract_last, preferred_element_type=jnp.float32)
    partial_in = partial_in + lax.dot_general(d_up, up_local, contract_last, preferred_element_type=jnp.float32)
    return grad_gate, grad_up, grad_down, partial_in


def rounded(values):
    return lax.optimization_barrier(values.astype(jnp.bfloat16)).astype(jnp.float32)


def reference(tokens, routes, mix_weights, w_gate, w_up, w_down, cotangent):
    blocks = N_EXPERT
    group_width = FF // N_TENSOR
    route_blocks = routes.reshape(blocks, 2 * TOK_DEV)
    onehot = (route_blocks[:, :, None] == jnp.arange(EXPERTS, dtype=jnp.int32)[None, None, :]).astype(jnp.int32)
    slot_rank = jnp.sum((jnp.cumsum(onehot, axis=1) - 1) * onehot, axis=2)
    anchor = jnp.arange(blocks, dtype=jnp.int32)[:, None]
    slot_index = ((route_blocks * blocks + anchor) * CAP + slot_rank).reshape(-1).astype(jnp.int32)
    all_rows = EXPERTS * blocks * CAP
    doubled = jnp.repeat(tokens, 2, axis=0)
    x_buffer = jnp.zeros((all_rows, D), jnp.bfloat16).at[slot_index].set(doubled)
    x_buffer = x_buffer.reshape(EXPERTS, blocks * CAP, D)
    scaled = (mix_weights[:, :, None] * cotangent.astype(jnp.float32)[:, None, :]).astype(jnp.bfloat16)
    g_buffer = jnp.zeros((all_rows, D), jnp.bfloat16).at[slot_index].set(scaled.reshape(2 * TOKENS, D))
    g_buffer = g_buffer.reshape(EXPERTS, blocks * CAP, D)

    def per_expert(operands):
        received, upstream, gate_all, up_all, down_all = operands
        out_total = jnp.zeros((blocks * CAP, D), jnp.float32)
        in_total = jnp.zeros((blocks * CAP, D), jnp.float32)
        gate_parts, up_parts, down_parts = [], [], []
        for member in range(N_TENSOR):
            low = member * group_width
            gate_local = gate_all[:, low:low + group_width]
            up_local = up_all[:, low:low + group_width]
            down_local = down_all[low:low + group_width, :]
            pre_gate, pre_up, hidden, partial_out = expert_forward(received, gate_local, up_local, down_local)
            out_total = out_total + rounded(partial_out)
            grad_gate, grad_up, grad_down, partial_in = expert_backward(
                received, upstream, pre_gate, pre_up, hidden, gate_local, up_local, down_local)
            in_total = in_total + rounded(partial_in)
            gate_parts.append(grad_gate)
            up_parts.append(grad_up)
            down_parts.append(grad_down)
        return (out_total.astype(jnp.bfloat16), in_total.astype(jnp.bfloat16),
                jnp.concatenate(gate_parts, axis=1), jnp.concatenate(up_parts, axis=1),
                jnp.concatenate(down_parts, axis=0))

    out_buf, in_buf, grad_gate, grad_up, grad_down = lax.map(
        per_expert, (x_buffer, g_buffer, w_gate, w_up, w_down))
    out_flat = out_buf.reshape(all_rows, D)
    in_flat = in_buf.reshape(all_rows, D)
    picked = out_flat[slot_index].astype(jnp.float32).reshape(TOKENS, 2, D)
    result = jnp.sum(picked * mix_weights[:, :, None], axis=1).astype(jnp.bfloat16)
    picked_in = in_flat[slot_index].astype(jnp.float32).reshape(TOKENS, 2, D)
    ones_weights = jnp.ones_like(mix_weights)
    grad_tokens = jnp.sum(picked_in * ones_weights[:, :, None], axis=1).astype(jnp.bfloat16)
    return result, grad_tokens, grad_gate, grad_up, grad_down
```

```python
import functools

import jax
import jax.numpy as jnp
from jax import lax
from jax.experimental import pallas as pl
from jax.experimental.pallas import tpu as pltpu
from jax.sharding import PartitionSpec as P

F32 = jnp.float32
BF16 = jnp.bfloat16
NN = (((1,), (0,)), ((), ()))
NT = (((1,), (1,)), ((), ()))
TN = (((0,), (0,)), ((), ()))


def dot(a, b, dims):
    return lax.dot_general(a, b, dims, preferred_element_type=F32)


def places(routes, experts, capacity):
    rows = routes.shape[0]
    first, second = routes[:, 0:1], routes[:, 1:2]
    lanes = lax.broadcasted_iota(jnp.int32, (rows, experts), 1)
    hot0 = (lanes == first).astype(F32)
    hot1 = (lanes == second).astype(F32)
    before = (
        lax.broadcasted_iota(jnp.int32, (rows, rows), 1)
        < lax.broadcasted_iota(jnp.int32, (rows, rows), 0)
    ).astype(F32)
    earlier = dot(before.astype(BF16), (hot0 + hot1).astype(BF16), NN)
    rank0 = jnp.sum(earlier * hot0, axis=1, keepdims=True)
    rank1 = jnp.sum((earlier + hot0) * hot1, axis=1, keepdims=True)
    return (
        first * capacity + rank0.astype(jnp.int32),
        second * capacity + rank1.astype(jnp.int32),
    )


def one_hot(place, width):
    lanes = lax.broadcasted_iota(jnp.int32, (place.shape[0], width), 1)
    return (lanes == place).astype(F32).astype(BF16)


def dispatch_kernel(capacity, experts, me, routes, mix, tokens, cotangent, x_out, g_out):
    place0, place1 = places(routes[...], experts, capacity)
    buffer_rows = experts * capacity
    pick0, pick1 = one_hot(place0, buffer_rows), one_hot(place1, buffer_rows)
    x_out[...] = dot(pick0 + pick1, tokens[...], TN).astype(BF16)
    cot = cotangent[...].astype(F32)
    weights = mix[...]
    scaled0 = (weights[:, 0:1] * cot).astype(BF16)
    scaled1 = (weights[:, 1:2] * cot).astype(BF16)
    g_out[...] = (dot(pick0, scaled0, TN) + dot(pick1, scaled1, TN)).astype(BF16)


def dispatch(member, routes, mix, tokens, cotangent, experts, capacity, parts):
    rows, width = tokens.shape[0], tokens.shape[1] // parts
    whole = lambda i, me: (0, 0)
    mine = lambda i, me: (0, me[0])
    out = jax.ShapeDtypeStruct((experts * capacity, width), BF16)
    return pl.pallas_call(
        functools.partial(dispatch_kernel, capacity, experts),
        grid_spec=pltpu.PrefetchScalarGridSpec(
            num_scalar_prefetch=1,
            grid=(1,),
            in_specs=[
                pl.BlockSpec((rows, 2), whole),
                pl.BlockSpec((rows, 2), whole),
                pl.BlockSpec((rows, width), mine),
                pl.BlockSpec((rows, width), mine),
            ],
            out_specs=[pl.BlockSpec((experts * capacity, width), whole)] * 2,
        ),
        out_shape=(out, out),
        compiler_params=pltpu.CompilerParams(vmem_limit_bytes=32 << 20),
        name="dispatch",
    )(member, routes, mix, tokens, cotangent)


def forward_kernel(parts, x, w_gate, w_up, w_down, pre_gate, pre_up, hidden, partial_out):
    width = x.shape[2]
    gate = up = None
    for t in range(parts):
        rows = pl.ds(t * width, width)
        g = dot(x[t], w_gate[0, rows, :], NN)
        u = dot(x[t], w_up[0, rows, :], NN)
        gate, up = (g, u) if gate is None else (gate + g, up + u)
    pre_gate[...] = gate
    pre_up[...] = up
    act = (gate / (1.0 + jnp.exp(-gate)) * up).astype(BF16)
    hidden[...] = act
    for t in range(parts):
        partial_out[t] = dot(act, w_down[0, :, pl.ds(t * width, width)], NN).astype(BF16)


def forward(x, w_gate, w_up, w_down, block):
    parts, rows, width = x.shape
    units = w_gate.shape[2]
    fixed = lambda i: (0, 0, 0)
    chunk = pl.BlockSpec((parts, block, width), lambda i: (0, i, 0))
    tall = pl.BlockSpec((block, units), lambda i: (i, 0))
    return pl.pallas_call(
        functools.partial(forward_kernel, parts),
        grid=(rows // block,),
        in_specs=[
            chunk,
            pl.BlockSpec(w_gate.shape, fixed),
            pl.BlockSpec(w_up.shape, fixed),
            pl.BlockSpec(w_down.shape, fixed),
        ],
        out_specs=[tall, tall, tall, chunk],
        out_shape=(
            jax.ShapeDtypeStruct((rows, units), F32),
            jax.ShapeDtypeStruct((rows, units), F32),
            jax.ShapeDtypeStruct((rows, units), BF16),
            jax.ShapeDtypeStruct((parts, rows, width), BF16),
        ),
        compiler_params=pltpu.CompilerParams(vmem_limit_bytes=48 << 20),
        cost_estimate=pl.CostEstimate(
            flops=6 * rows * parts * width * units, bytes_accessed=12 << 20, transcendentals=rows * units
        ),
        name="forward",
    )(x, w_gate, w_up, w_down)


def backward_kernel(parts, g, pre_gate, pre_up, w_gate, w_up, w_down, d_gate, d_up, partial_in):
    width = g.shape[2]
    d_hidden = None
    for t in range(parts):
        part = dot(g[t], w_down[0, :, pl.ds(t * width, width)], NT)
        d_hidden = part if d_hidden is None else d_hidden + part
    gate, up = pre_gate[...], pre_up[...]
    sigma = 1.0 / (1.0 + jnp.exp(-gate))
    dg = (d_hidden * up * sigma * (1.0 + gate * (1.0 - sigma))).astype(BF16)
    du = (d_hidden * gate * sigma).astype(BF16)
    d_gate[...] = dg
    d_up[...] = du
    for t in range(parts):
        rows = pl.ds(t * width, width)
        partial_in[t] = (dot(dg, w_gate[0, rows, :], NT) + dot(du, w_up[0, rows, :], NT)).astype(BF16)


def backward(g, pre_gate, pre_up, w_gate, w_up, w_down, block):
    parts, rows, width = g.shape
    units = w_gate.shape[2]
    fixed = lambda i: (0, 0, 0)
    chunk = pl.BlockSpec((parts, block, width), lambda i: (0, i, 0))
    tall = pl.BlockSpec((block, units), lambda i: (i, 0))
    return pl.pallas_call(
        functools.partial(backward_kernel, parts),
        grid=(rows // block,),
        in_specs=[
            chunk,
            tall,
            tall,
            pl.BlockSpec(w_gate.shape, fixed),
            pl.BlockSpec(w_up.shape, fixed),
            pl.BlockSpec(w_down.shape, fixed),
        ],
        out_specs=[tall, tall, chunk],
        out_shape=(
            jax.ShapeDtypeStruct((rows, units), BF16),
            jax.ShapeDtypeStruct((rows, units), BF16),
            jax.ShapeDtypeStruct((parts, rows, width), BF16),
        ),
        compiler_params=pltpu.CompilerParams(vmem_limit_bytes=48 << 20),
        cost_estimate=pl.CostEstimate(
            flops=6 * rows * parts * width * units, bytes_accessed=13 << 20, transcendentals=rows * units
        ),
        name="backward",
    )(g, pre_gate, pre_up, w_gate, w_up, w_down)


def weights_kernel(x, g, hidden, d_gate, d_up, grad_gate, grad_up, grad_down):
    grad_gate[0] = dot(x[0], d_gate[...], TN)
    grad_up[0] = dot(x[0], d_up[...], TN)
    grad_down[0] = dot(hidden[...], g[0], TN)


def weight_grads(x, g, hidden, d_gate, d_up):
    parts, rows, width = x.shape
    units = hidden.shape[1]
    fixed = pl.BlockSpec((rows, units), lambda t: (0, 0))
    chunk = pl.BlockSpec((1, rows, width), lambda t: (t, 0, 0))
    tall = pl.BlockSpec((1, width, units), lambda t: (0, t, 0))
    return pl.pallas_call(
        weights_kernel,
        grid=(parts,),
        in_specs=[chunk, chunk, fixed, fixed, fixed],
        out_specs=[tall, tall, pl.BlockSpec((1, units, width), lambda t: (0, 0, t))],
        out_shape=(
            jax.ShapeDtypeStruct((1, parts * width, units), F32),
            jax.ShapeDtypeStruct((1, parts * width, units), F32),
            jax.ShapeDtypeStruct((1, units, parts * width), F32),
        ),
        compiler_params=pltpu.CompilerParams(vmem_limit_bytes=48 << 20),
        cost_estimate=pl.CostEstimate(
            flops=6 * rows * parts * width * units, bytes_accessed=13 << 20, transcendentals=0
        ),
        name="weight_grads",
    )(x, g, hidden, d_gate, d_up)


def combine_kernel(capacity, experts, weighted, routes, mix, back, out):
    place0, place1 = places(routes[...], experts, capacity)
    values = back[...]
    first = dot(one_hot(place0, values.shape[0]), values, NN)
    second = dot(one_hot(place1, values.shape[0]), values, NN)
    if weighted:
        first = first * mix[:, 0:1]
        second = second * mix[:, 1:2]
    out[...] = (first + second).astype(BF16)


def combine(routes, mix, back, experts, capacity, weighted):
    return pl.pallas_call(
        functools.partial(combine_kernel, capacity, experts, weighted),
        out_shape=jax.ShapeDtypeStruct((routes.shape[0], back.shape[1]), BF16),
        compiler_params=pltpu.CompilerParams(vmem_limit_bytes=32 << 20),
        name="combine",
    )(routes, mix, back)


def exchange(values, experts, capacity):
    width = values.shape[1]
    moved = lax.all_to_all(
        values.reshape(experts, capacity, width), "expert", split_axis=0, concat_axis=0, tiled=True
    )
    return moved.reshape(experts * capacity, width)


def shards(tokens, routes, mix_weights, w_gate, w_up, w_down, cotangent):
    experts = lax.axis_size("expert")
    parts = lax.axis_size("tensor")
    capacity = 4 * tokens.shape[0] // experts
    block = 256
    member = lax.axis_index("tensor").astype(jnp.int32).reshape(1)
    x_sent, g_sent = dispatch(
        member, routes, mix_weights, tokens, cotangent, experts, capacity, parts
    )
    x_mine = exchange(x_sent, experts, capacity)
    x = lax.all_gather(x_mine, "tensor")
    g_mine = exchange(g_sent, experts, capacity)
    g = lax.all_gather(g_mine, "tensor")
    pre_gate, pre_up, hidden, partial_out = forward(x, w_gate, w_up, w_down, block)
    out_mine = lax.psum_scatter(partial_out, "tensor", scatter_dimension=0, tiled=False)
    d_gate, d_up, partial_in = backward(g, pre_gate, pre_up, w_gate, w_up, w_down, block)
    in_mine = lax.psum_scatter(partial_in, "tensor", scatter_dimension=0, tiled=False)
    grad_gate, grad_up, grad_down = weight_grads(x, g, hidden, d_gate, d_up)
    out_back = exchange(out_mine, experts, capacity)
    result = combine(routes, mix_weights, out_back, experts, capacity, True)
    result = lax.all_gather(result, "tensor", axis=1, tiled=True)
    in_back = exchange(in_mine, experts, capacity)
    grad_tokens = combine(routes, mix_weights, in_back, experts, capacity, False)
    grad_tokens = lax.all_gather(grad_tokens, "tensor", axis=1, tiled=True)
    return (result, grad_tokens, grad_gate, grad_up, grad_down)


def solution(mesh):
    in_specs = (
        P("expert", None),
        P("expert", None),
        P("expert", None),
        P("expert", None, "tensor"),
        P("expert", None, "tensor"),
        P("expert", "tensor", None),
        P("expert", None),
    )
    out_specs = (
        P("expert", None),
        P("expert", None),
        P("expert", None, "tensor"),
        P("expert", None, "tensor"),
        P("expert", "tensor", None),
    )
    return jax.shard_map(shards, mesh=mesh, in_specs=in_specs, out_specs=out_specs, check_vma=False)
```

```python
import functools

import jax
import jax.numpy as jnp
from jax import lax
from jax.experimental import pallas as pl
from jax.experimental.pallas import tpu as pltpu
from jax.sharding import PartitionSpec as P

F32 = jnp.float32
BF16 = jnp.bfloat16
NN = (((1,), (0,)), ((), ()))
NT = (((1,), (1,)), ((), ()))
TN = (((0,), (0,)), ((), ()))


def dot(a, b, dims):
    return lax.dot_general(a, b, dims, preferred_element_type=F32)


VMEM = pl.BlockSpec(memory_space=pltpu.VMEM)
SMEM = pl.BlockSpec(memory_space=pltpu.SMEM)
ANY = pl.BlockSpec(memory_space=pl.ANY)
HBM = pl.BlockSpec(memory_space=pltpu.HBM)
TOKEN = jax.ShapeDtypeStruct((8, 128), F32)


def one_hot(place, height):
    lines = lax.broadcasted_iota(jnp.int32, (height, place.shape[1]), 0)
    return (lines == place).astype(F32).astype(BF16)


def dispatch_kernel(capacity, experts, me, routes_in, mix_in, tokens_in, cotangent_in, sent, info, *scratch):
    routes, mix, tokens, cotangent, sems = scratch
    rows, width = tokens.shape
    mine = pl.ds(pl.multiple_of(me[0] * width, width), width)
    fetches = [
        pltpu.make_async_copy(source, slot, sems.at[i])
        for i, (source, slot) in enumerate(
            [
                (routes_in, routes),
                (mix_in, mix),
                (tokens_in.at[:, mine], tokens),
                (cotangent_in.at[:, mine], cotangent),
            ]
        )
    ]
    for fetch in fetches:
        fetch.start()
    for fetch in fetches:
        fetch.wait()
    first, second = routes[0:1, :], routes[1:2, :]
    lines = lax.broadcasted_iota(jnp.int32, (experts, rows), 0)
    hot0 = (lines == first).astype(F32)
    hot1 = (lines == second).astype(F32)
    before = lax.broadcasted_iota(jnp.int32, (rows, rows), 0) < lax.broadcasted_iota(jnp.int32, (rows, rows), 1)
    earlier = dot((hot0 + hot1).astype(BF16), before.astype(F32).astype(BF16), NN)
    rank0 = jnp.sum(earlier * hot0, axis=0, keepdims=True)
    rank1 = jnp.sum((earlier + hot0) * hot1, axis=0, keepdims=True)
    place0 = first * capacity + rank0.astype(jnp.int32)
    place1 = second * capacity + rank1.astype(jnp.int32)
    buffer_rows = experts * capacity
    pick0, pick1 = one_hot(place0, buffer_rows), one_hot(place1, buffer_rows)
    columns = jnp.concatenate(
        [place0.astype(F32), place1.astype(F32), mix[...], jnp.zeros((4, rows), F32)], axis=0
    ).T
    info[...] = columns
    x = dot(pick0 + pick1, tokens[...], NN).astype(BF16)
    sent[:, pl.ds(0, capacity), :] = x.reshape(experts, capacity, x.shape[1])
    cot = cotangent[...].astype(F32)
    scaled0 = (columns[:, 2:3] * cot).astype(BF16)
    scaled1 = (columns[:, 3:4] * cot).astype(BF16)
    g = (dot(pick0, scaled0, NN) + dot(pick1, scaled1, NN)).astype(BF16)
    sent[:, pl.ds(capacity, capacity), :] = g.reshape(experts, capacity, g.shape[1])


def dispatch(me, routes, mix, tokens, cotangent, experts, capacity, parts):
    rows, width = tokens.shape[0], tokens.shape[1] // parts
    return pl.pallas_call(
        functools.partial(dispatch_kernel, capacity, experts),
        in_specs=[SMEM] + [HBM] * 4,
        out_specs=[VMEM] * 2,
        out_shape=(
            jax.ShapeDtypeStruct((experts, 2 * capacity, width), BF16),
            jax.ShapeDtypeStruct((rows, 8), F32),
        ),
        scratch_shapes=[
            pltpu.VMEM((2, rows), jnp.int32),
            pltpu.VMEM((2, rows), F32),
            pltpu.VMEM((rows, width), BF16),
            pltpu.VMEM((rows, width), BF16),
            pltpu.SemaphoreType.DMA((4,)),
        ],
        compiler_params=pltpu.CompilerParams(vmem_limit_bytes=60 << 20),
        name="dispatch",
    )(me, routes.T, mix.T, tokens, cotangent)


def split_kernel(start, capacity, received, after, *halves):
    groups = received.shape[0] // len(halves)
    for h, half in enumerate(halves):
        half[...] = received[pl.ds(h * groups, groups), pl.ds(start, capacity), :]


def split(received, start, capacity, after):
    experts, _, width = received.shape
    half = jax.ShapeDtypeStruct((experts // 2, capacity, width), BF16)
    out = pl.pallas_call(
        functools.partial(split_kernel, start, capacity),
        in_specs=[VMEM, VMEM],
        out_specs=[VMEM] * 2,
        out_shape=[half] * 2,
        compiler_params=pltpu.CompilerParams(vmem_limit_bytes=2 << 20),
        name="split",
    )(received, after)
    return [v.reshape(experts // 2 * capacity, width) for v in out]


def column_block(me, shift, parts, width):
    owner = lax.rem(me[0] + (parts - shift), parts)
    return pl.multiple_of(owner * width, width)


def forward_kernel(parts, halves, me, *refs):
    x = refs[: parts * halves]
    w_gate, w_up, w_down = refs[parts * halves : parts * halves + 3]
    pre_gate, pre_up, hidden = refs[parts * halves + 3 : parts * halves + 6]
    partial_out = refs[parts * halves + 6 :]
    rows, width = x[0].shape
    for h in range(halves):
        gate = up = None
        for shift in range(parts):
            block = x[shift * halves + h][...]
            lines = pl.ds(column_block(me, shift, parts, width), width)
            g = dot(block, w_gate[0, lines, :], NN)
            u = dot(block, w_up[0, lines, :], NN)
            gate, up = (g, u) if gate is None else (gate + g, up + u)
        part = pl.ds(h * rows, rows)
        pre_gate[part, :] = gate
        pre_up[part, :] = up
        act = (gate / (1.0 + jnp.exp(-gate)) * up).astype(BF16)
        hidden[part, :] = act
        for shift in range(parts):
            columns = pl.ds(column_block(me, parts - shift, parts, width), width)
            partial_out[shift * halves + h][...] = dot(act, w_down[0, :, columns], NN).astype(BF16)


def forward(me, x, w_gate, w_up, w_down):
    parts, halves = len(x), len(x[0])
    rows, width = x[0][0].shape
    units = w_gate.shape[2]
    n = parts * halves
    out = pl.pallas_call(
        functools.partial(forward_kernel, parts, halves),
        in_specs=[SMEM] + [VMEM] * (n + 3),
        out_specs=[VMEM] * (n + 3),
        out_shape=[jax.ShapeDtypeStruct((halves * rows, units), F32)] * 2
        + [jax.ShapeDtypeStruct((halves * rows, units), BF16)]
        + [jax.ShapeDtypeStruct((rows, width), BF16)] * n,
        compiler_params=pltpu.CompilerParams(vmem_limit_bytes=10 << 20),
        cost_estimate=pl.CostEstimate(
            flops=6 * halves * rows * parts * width * units, bytes_accessed=12 << 20, transcendentals=halves * rows * units
        ),
        name="forward",
    )(me, *[piece for chunk in x for piece in chunk], w_gate, w_up, w_down)
    return out[0], out[1], out[2], [out[3 + i * halves : 3 + (i + 1) * halves] for i in range(parts)]


def backward_kernel(parts, halves, me, *refs):
    n = parts * halves
    g = refs[:n]
    pre_gate, pre_up, w_gate, w_up, w_down = refs[n : n + 5]
    d_gate, d_up, done = refs[n + 5 : n + 8]
    partial_in = refs[n + 8 :]
    done[...] = jnp.zeros(done.shape, F32)
    rows, width = g[0].shape
    for h in range(halves):
        d_hidden = None
        for shift in range(parts):
            columns = pl.ds(column_block(me, shift, parts, width), width)
            part = dot(g[shift * halves + h][...], w_down[0, :, columns], NT)
            d_hidden = part if d_hidden is None else d_hidden + part
        mine = pl.ds(h * rows, rows)
        gate, up = pre_gate[mine, :], pre_up[mine, :]
        sigma = 1.0 / (1.0 + jnp.exp(-gate))
        dg = (d_hidden * up * sigma * (1.0 + gate * (1.0 - sigma))).astype(BF16)
        du = (d_hidden * gate * sigma).astype(BF16)
        d_gate[mine, :] = dg
        d_up[mine, :] = du
        for shift in range(parts):
            lines = pl.ds(column_block(me, parts - shift, parts, width), width)
            partial_in[shift * halves + h][...] = (
                dot(dg, w_gate[0, lines, :], NT) + dot(du, w_up[0, lines, :], NT)
            ).astype(BF16)


def backward(me, g, pre_gate, pre_up, w_gate, w_up, w_down):
    parts, halves = len(g), len(g[0])
    rows, width = g[0][0].shape
    units = w_gate.shape[2]
    n = parts * halves
    out = pl.pallas_call(
        functools.partial(backward_kernel, parts, halves),
        in_specs=[SMEM] + [VMEM] * (n + 5),
        out_specs=[VMEM] * (n + 3),
        out_shape=[jax.ShapeDtypeStruct((halves * rows, units), BF16)] * 2
        + [TOKEN]
        + [jax.ShapeDtypeStruct((rows, width), BF16)] * n,
        compiler_params=pltpu.CompilerParams(vmem_limit_bytes=10 << 20),
        cost_estimate=pl.CostEstimate(
            flops=6 * halves * rows * parts * width * units, bytes_accessed=12 << 20, transcendentals=halves * rows * units
        ),
        name="backward",
    )(me, *[piece for chunk in g for piece in chunk], pre_gate, pre_up, w_gate, w_up, w_down)
    return out[0], out[1], out[2], [out[3 + i * halves : 3 + (i + 1) * halves] for i in range(parts)]


def weights_kernel(parts, halves, me, *refs):
    n = parts * halves
    sources = refs[: 2 * n + 3]
    grad_gate, grad_up, grad_down, done = refs[2 * n + 4 : 2 * n + 8]
    x, g, units3, tall, wide, in_sems, out_sems = refs[2 * n + 8 :]
    hidden, d_gate, d_up = units3.at[0], units3.at[1], units3.at[2]
    rows, width = x.shape[1:]
    slots = [x.at[i] for i in range(n)] + [g.at[i] for i in range(n)] + [hidden, d_gate, d_up]
    fetches = [
        pltpu.make_async_copy(source, slot, in_sems.at[i]) for i, (source, slot) in enumerate(zip(sources, slots))
    ]
    tail = 2 * n
    order = [tail + 1, tail + 2]
    for shift in range(parts):
        order += [shift * halves + h for h in range(halves)]
    order += [tail]
    for shift in range(parts):
        order += [n + shift * halves + h for h in range(halves)]
    for i in order:
        fetches[i].start()
    done[...] = jnp.zeros(done.shape, F32)
    copies = []

    def send(kind, shift, slot, target):
        copy = pltpu.make_async_copy(slot, target, out_sems.at[kind * parts + shift])
        copy.start()
        copies.append(copy)

    def product(left, right):
        total = None
        for h in range(halves):
            part = dot(left(h), right(h), TN)
            total = part if total is None else total + part
        return total

    part = lambda ref: (lambda h: ref[pl.ds(h * rows, rows), :])
    fetches[tail + 1].wait()
    fetches[tail + 2].wait()
    for shift in range(parts):
        where = pl.ds(column_block(me, shift, parts, width), width)
        for h in range(halves):
            fetches[shift * halves + h].wait()
        block = lambda h: x[shift * halves + h]
        tall[shift] = product(block, part(d_gate))
        send(0, shift, tall.at[shift], grad_gate.at[0, where, :])
        tall[parts + shift] = product(block, part(d_up))
        send(1, shift, tall.at[parts + shift], grad_up.at[0, where, :])
    fetches[tail].wait()
    for shift in range(parts):
        where = pl.ds(column_block(me, shift, parts, width), width)
        for h in range(halves):
            fetches[n + shift * halves + h].wait()
        wide[shift] = product(part(hidden), lambda h: g[shift * halves + h])
        send(2, shift, wide.at[shift], grad_down.at[0, :, where])
    for copy in copies:
        copy.wait()


def weight_grads(me, x, g, hidden, d_gate, d_up, after):
    parts, halves = len(x), len(x[0])
    rows, width = x[0][0].shape
    units = hidden.shape[1]
    n = parts * halves
    return pl.pallas_call(
        functools.partial(weights_kernel, parts, halves),
        in_specs=[SMEM] + [HBM] * (2 * n + 3) + [VMEM],
        out_specs=[HBM] * 3 + [VMEM],
        out_shape=(
            jax.ShapeDtypeStruct((1, parts * width, units), F32),
            jax.ShapeDtypeStruct((1, parts * width, units), F32),
            jax.ShapeDtypeStruct((1, units, parts * width), F32),
            TOKEN,
        ),
        scratch_shapes=[
            pltpu.VMEM((n, rows, width), BF16),
            pltpu.VMEM((n, rows, width), BF16),
            pltpu.VMEM((3, halves * rows, units), BF16),
            pltpu.VMEM((2 * parts, width, units), F32),
            pltpu.VMEM((parts, units, width), F32),
            pltpu.SemaphoreType.DMA((2 * n + 3,)),
            pltpu.SemaphoreType.DMA((3 * parts,)),
        ],
        compiler_params=pltpu.CompilerParams(vmem_limit_bytes=58 << 20),
        cost_estimate=pl.CostEstimate(
            flops=6 * halves * rows * parts * width * units, bytes_accessed=13 << 20, transcendentals=0
        ),
        name="weight_grads",
    )(me, *[v for c in x for v in c], *[v for c in g for v in c], hidden, d_gate, d_up, after)


def total_kernel(halves, *refs):
    out, done = refs[-2:]
    terms = len(refs[:-3]) // halves
    done[...] = jnp.zeros(done.shape, F32)
    rows = refs[0].shape[0]
    step = 32

    @pl.loop(0, rows // step)
    def _(i):
        here = pl.ds(pl.multiple_of(i * step, step), step)
        for h in range(halves):
            total = refs[h * terms][here, :].astype(F32)
            for k in range(1, terms):
                total = total + refs[h * terms + k][here, :].astype(F32)
            out[pl.ds(pl.multiple_of(h * rows + i * step, step), step), :] = total.astype(BF16)


def totals(groups, after):
    rows, width = groups[0][0].shape
    return pl.pallas_call(
        functools.partial(total_kernel, len(groups)),
        in_specs=[VMEM] * sum(map(len, groups)) + [VMEM],
        out_specs=[VMEM] * 2,
        out_shape=(jax.ShapeDtypeStruct((len(groups) * rows, width), BF16), TOKEN),
        compiler_params=pltpu.CompilerParams(vmem_limit_bytes=2 << 20),
        name="totals",
    )(*[v for group in groups for v in group], after)


def assemble_kernel(parts, me, *refs):
    out, done, sems = refs[parts:]
    done[...] = jnp.zeros(done.shape, F32)
    width = refs[0].shape[1]
    copies = []
    for shift in range(parts):
        columns = pl.ds(column_block(me, shift, parts, width), width)
        copies.append(pltpu.make_async_copy(refs[shift], out.at[:, columns], sems.at[shift]))
        copies[-1].start()
    for copy in copies:
        copy.wait()


def assemble(me, chunks):
    rows, width = chunks[0].shape
    parts = len(chunks)
    return pl.pallas_call(
        functools.partial(assemble_kernel, parts),
        in_specs=[SMEM] + [VMEM] * parts,
        out_specs=[HBM, VMEM],
        out_shape=(jax.ShapeDtypeStruct((rows, width * parts), BF16), TOKEN),
        scratch_shapes=[pltpu.SemaphoreType.DMA((parts,))],
        compiler_params=pltpu.CompilerParams(vmem_limit_bytes=2 << 20),
        name="assemble",
    )(me, *chunks)


def combine_kernel(weighted, info, back, *refs):
    out = refs[-1]
    values = back[...]
    columns = info[...]
    lanes = lax.broadcasted_iota(jnp.int32, (columns.shape[0], values.shape[0]), 1)
    picked = []
    for k in range(2):
        hot = (lanes == columns[:, k : k + 1].astype(jnp.int32)).astype(F32).astype(BF16)
        row = dot(hot, values, NN)
        picked.append(row * columns[:, 2 + k : 3 + k] if weighted else row)
    out[...] = (picked[0] + picked[1]).astype(BF16)


def combine(info, back, weighted, after):
    return pl.pallas_call(
        functools.partial(combine_kernel, weighted),
        in_specs=[VMEM] * (2 + len(after)),
        out_specs=VMEM,
        out_shape=jax.ShapeDtypeStruct((info.shape[0], back.shape[1]), BF16),
        compiler_params=pltpu.CompilerParams(vmem_limit_bytes=8 << 20),
        name="combine",
    )(info, back, *after)


def swap_blocks(values):
    return lax.all_to_all(values, "expert", split_axis=0, concat_axis=0, tiled=True)


def send_back(values, experts, capacity):
    rows, width = values.shape
    return swap_blocks(values.reshape(experts, capacity, width)).reshape(rows, width)


def shift_by(values, step):
    size = lax.axis_size("tensor")
    return lax.ppermute(values, "tensor", [(i, (i + step) % size) for i in range(size)])


def gather_ring(top, bottom):
    left_top = shift_by(top, 1)
    right_bottom = shift_by(bottom, -1)
    left_bottom = shift_by(bottom, 1)
    right_top = shift_by(top, -1)
    far_top = shift_by(left_top, 1)
    far_bottom = shift_by(right_bottom, -1)
    return [(top, bottom), (left_top, left_bottom), (far_top, far_bottom), (right_top, right_bottom)]


def add(a, b):
    return (a.astype(F32) + b.astype(F32)).astype(BF16)


def scatter_ring(chunks):
    own, right, far, left = chunks
    far_top = shift_by(far[0], -1)
    far_bottom = shift_by(far[1], 1)
    from_left_top = shift_by(right[0], 1)
    from_right_bottom = shift_by(left[1], -1)
    from_right_top = shift_by(add(left[0], far_top), -1)
    from_left_bottom = shift_by(add(right[1], far_bottom), 1)
    return [
        (own[0], from_left_top, from_right_top),
        (own[1], from_right_bottom, from_left_bottom),
    ]


def gather_columns(me, values):
    far = shift_by(values, 2)
    left = shift_by(values, 1)
    right = shift_by(values, -1)
    return assemble(me, [values, left, far, right])


def shards(tokens, routes, mix_weights, w_gate, w_up, w_down, cotangent):
    experts = lax.axis_size("expert")
    parts = lax.axis_size("tensor")
    capacity = 4 * tokens.shape[0] // experts
    me = lax.axis_index("tensor").astype(jnp.int32).reshape(1)
    sent, info = dispatch(me, routes, mix_weights, tokens, cotangent, experts, capacity, parts)
    received = swap_blocks(sent)
    x = gather_ring(*split(received, 0, capacity, info))
    g = gather_ring(*split(received, capacity, capacity, x[1][0]))
    pre_gate, pre_up, hidden, partial_out = forward(me, x, w_gate, w_up, w_down)
    out_terms = scatter_ring(partial_out)
    d_gate, d_up, after_backward, partial_in = backward(me, g, pre_gate, pre_up, w_gate, w_up, w_down)
    out_mine, _ = totals(out_terms, after_backward)
    out_back = send_back(out_mine, experts, capacity)
    in_mine, after_sums = totals(scatter_ring(partial_in), after_backward)
    in_back = send_back(in_mine, experts, capacity)
    grad_gate, grad_up, grad_down, after_weights = weight_grads(me, x, g, hidden, d_gate, d_up, after_sums)
    result, after_result = gather_columns(me, combine(info, out_back, True, [after_sums]))
    grad_tokens, _ = gather_columns(me, combine(info, in_back, False, [after_weights, after_result]))
    return (result, grad_tokens, grad_gate, grad_up, grad_down)


def solution(mesh):
    in_specs = (
        P("expert", None),
        P("expert", None),
        P("expert", None),
        P("expert", None, "tensor"),
        P("expert", None, "tensor"),
        P("expert", "tensor", None),
        P("expert", None),
    )
    out_specs = (
        P("expert", None),
        P("expert", None),
        P("expert", None, "tensor"),
        P("expert", None, "tensor"),
        P("expert", "tensor", None),
    )
    return jax.shard_map(shards, mesh=mesh, in_specs=in_specs, out_specs=out_specs, check_vma=False)
```

```python
import functools

import jax
import jax.numpy as jnp
from jax import lax
from jax.experimental import pallas as pl
from jax.experimental.pallas import tpu as pltpu
from jax.sharding import PartitionSpec as P

F32 = jnp.float32
BF16 = jnp.bfloat16
NN = (((1,), (0,)), ((), ()))
NT = (((1,), (1,)), ((), ()))
TN = (((0,), (0,)), ((), ()))


def dot(a, b, dims):
    return lax.dot_general(a, b, dims, preferred_element_type=F32)


VMEM = pl.BlockSpec(memory_space=pltpu.VMEM)
SMEM = pl.BlockSpec(memory_space=pltpu.SMEM)
ANY = pl.BlockSpec(memory_space=pl.ANY)
HBM = pl.BlockSpec(memory_space=pltpu.HBM)
TOKEN = jax.ShapeDtypeStruct((8, 128), F32)


def one_hot(place, height):
    lines = lax.broadcasted_iota(jnp.int32, (height, place.shape[1]), 0)
    return (lines == place).astype(F32).astype(BF16)


def dispatch_kernel(capacity, experts, me, routes_in, mix_in, tokens_in, cotangent_in, sent, info, *scratch):
    routes, mix, tokens, cotangent, sems = scratch
    rows, width = tokens.shape
    mine = pl.ds(pl.multiple_of(me[0] * width, width), width)
    fetches = [
        pltpu.make_async_copy(source, slot, sems.at[i])
        for i, (source, slot) in enumerate(
            [
                (routes_in, routes),
                (mix_in, mix),
                (tokens_in.at[:, mine], tokens),
                (cotangent_in.at[:, mine], cotangent),
            ]
        )
    ]
    for fetch in fetches:
        fetch.start()
    for fetch in fetches:
        fetch.wait()
    first, second = routes[0:1, :], routes[1:2, :]
    lines = lax.broadcasted_iota(jnp.int32, (experts, rows), 0)
    hot0 = (lines == first).astype(F32)
    hot1 = (lines == second).astype(F32)
    before = lax.broadcasted_iota(jnp.int32, (rows, rows), 0) < lax.broadcasted_iota(jnp.int32, (rows, rows), 1)
    earlier = dot((hot0 + hot1).astype(BF16), before.astype(F32).astype(BF16), NN)
    rank0 = jnp.sum(earlier * hot0, axis=0, keepdims=True)
    rank1 = jnp.sum((earlier + hot0) * hot1, axis=0, keepdims=True)
    place0 = first * capacity + rank0.astype(jnp.int32)
    place1 = second * capacity + rank1.astype(jnp.int32)
    buffer_rows = experts * capacity
    pick0, pick1 = one_hot(place0, buffer_rows), one_hot(place1, buffer_rows)
    columns = jnp.concatenate(
        [place0.astype(F32), place1.astype(F32), mix[...], jnp.zeros((4, rows), F32)], axis=0
    ).T
    info[...] = columns
    x = dot(pick0 + pick1, tokens[...], NN).astype(BF16)
    sent[:, pl.ds(0, capacity), :] = x.reshape(experts, capacity, x.shape[1])
    cot = cotangent[...].astype(F32)
    scaled0 = (columns[:, 2:3] * cot).astype(BF16)
    scaled1 = (columns[:, 3:4] * cot).astype(BF16)
    g = (dot(pick0, scaled0, NN) + dot(pick1, scaled1, NN)).astype(BF16)
    sent[:, pl.ds(capacity, capacity), :] = g.reshape(experts, capacity, g.shape[1])


def dispatch(me, routes, mix, tokens, cotangent, experts, capacity, parts):
    rows, width = tokens.shape[0], tokens.shape[1] // parts
    return pl.pallas_call(
        functools.partial(dispatch_kernel, capacity, experts),
        in_specs=[SMEM] + [HBM] * 4,
        out_specs=[VMEM] * 2,
        out_shape=(
            jax.ShapeDtypeStruct((experts, 2 * capacity, width), BF16),
            jax.ShapeDtypeStruct((rows, 8), F32),
        ),
        scratch_shapes=[
            pltpu.VMEM((2, rows), jnp.int32),
            pltpu.VMEM((2, rows), F32),
            pltpu.VMEM((rows, width), BF16),
            pltpu.VMEM((rows, width), BF16),
            pltpu.SemaphoreType.DMA((4,)),
        ],
        compiler_params=pltpu.CompilerParams(vmem_limit_bytes=60 << 20),
        name="dispatch",
    )(me, routes.T, mix.T, tokens, cotangent)


def pick_kernel(start, received, after, out):
    out[...] = received[:, pl.ds(start, out.shape[1]), :]


def pick(received, start, capacity, after):
    experts, _, width = received.shape
    return pl.pallas_call(
        functools.partial(pick_kernel, start),
        in_specs=[VMEM, VMEM],
        out_specs=VMEM,
        out_shape=jax.ShapeDtypeStruct((experts, capacity, width), BF16),
        compiler_params=pltpu.CompilerParams(vmem_limit_bytes=2 << 20),
        name="pick",
    )(received, after).reshape(experts * capacity, width)


def column_block(me, shift, parts, width):
    owner = lax.rem(me[0] + (parts - shift), parts)
    return pl.multiple_of(owner * width, width)


def by_chunk(refs, counts, halves):
    chunks, at = [], 0
    for count in counts:
        if count == 1:
            rows = refs[at].shape[0] // halves
            chunks.append([refs[at].at[pl.ds(h * rows, rows), :] for h in range(halves)])
        else:
            chunks.append(list(refs[at : at + count]))
        at += count
    return chunks


def forward_kernel(parts, halves, counts, me, *refs):
    n = sum(counts)
    x = by_chunk(refs[:n], counts, halves)
    w_gate, w_up, w_down = refs[n : n + 3]
    pre_gate, pre_up, hidden = refs[n + 3 : n + 6]
    partial_out = refs[n + 6 :]
    rows, width = partial_out[0].shape
    for h in range(halves):
        gate = up = None
        for shift in range(parts):
            block = x[shift][h][...]
            lines = pl.ds(column_block(me, shift, parts, width), width)
            g = dot(block, w_gate[0, lines, :], NN)
            u = dot(block, w_up[0, lines, :], NN)
            gate, up = (g, u) if gate is None else (gate + g, up + u)
        part = pl.ds(h * rows, rows)
        pre_gate[part, :] = gate
        pre_up[part, :] = up
        act = (gate / (1.0 + jnp.exp(-gate)) * up).astype(BF16)
        hidden[part, :] = act
        for shift in range(parts):
            columns = pl.ds(column_block(me, parts - shift, parts, width), width)
            partial_out[shift * halves + h][...] = dot(act, w_down[0, :, columns], NN).astype(BF16)


def forward(me, x, w_gate, w_up, w_down):
    parts, halves, counts = len(x), 2, tuple(map(len, x))
    rows, width = x[0][0].shape[0] * counts[0] // halves, x[0][0].shape[1]
    units = w_gate.shape[2]
    n = parts * halves
    out = pl.pallas_call(
        functools.partial(forward_kernel, parts, halves, counts),
        in_specs=[SMEM] + [VMEM] * (sum(counts) + 3),
        out_specs=[VMEM] * (n + 3),
        out_shape=[jax.ShapeDtypeStruct((halves * rows, units), F32)] * 2
        + [jax.ShapeDtypeStruct((halves * rows, units), BF16)]
        + [jax.ShapeDtypeStruct((rows, width), BF16)] * n,
        compiler_params=pltpu.CompilerParams(vmem_limit_bytes=10 << 20),
        cost_estimate=pl.CostEstimate(
            flops=6 * halves * rows * parts * width * units, bytes_accessed=12 << 20, transcendentals=halves * rows * units
        ),
        name="forward",
    )(me, *[piece for chunk in x for piece in chunk], w_gate, w_up, w_down)
    return out[0], out[1], out[2], [out[3 + i * halves : 3 + (i + 1) * halves] for i in range(parts)]


def backward_kernel(parts, halves, counts, me, *refs):
    n = sum(counts)
    g = by_chunk(refs[:n], counts, halves)
    pre_gate, pre_up, w_gate, w_up, w_down = refs[n : n + 5]
    d_gate, d_up, done = refs[n + 5 : n + 8]
    partial_in = refs[n + 8 :]
    done[...] = jnp.zeros(done.shape, F32)
    rows, width = partial_in[0].shape
    for h in range(halves):
        d_hidden = None
        for shift in range(parts):
            columns = pl.ds(column_block(me, shift, parts, width), width)
            part = dot(g[shift][h][...], w_down[0, :, columns], NT)
            d_hidden = part if d_hidden is None else d_hidden + part
        mine = pl.ds(h * rows, rows)
        gate, up = pre_gate[mine, :], pre_up[mine, :]
        sigma = 1.0 / (1.0 + jnp.exp(-gate))
        dg = (d_hidden * up * sigma * (1.0 + gate * (1.0 - sigma))).astype(BF16)
        du = (d_hidden * gate * sigma).astype(BF16)
        d_gate[mine, :] = dg
        d_up[mine, :] = du
        for shift in range(parts):
            lines = pl.ds(column_block(me, parts - shift, parts, width), width)
            partial_in[shift * halves + h][...] = (
                dot(dg, w_gate[0, lines, :], NT) + dot(du, w_up[0, lines, :], NT)
            ).astype(BF16)


def backward(me, g, pre_gate, pre_up, w_gate, w_up, w_down):
    parts, halves, counts = len(g), 2, tuple(map(len, g))
    rows, width = g[0][0].shape[0] * counts[0] // halves, g[0][0].shape[1]
    units = w_gate.shape[2]
    n = parts * halves
    out = pl.pallas_call(
        functools.partial(backward_kernel, parts, halves, counts),
        in_specs=[SMEM] + [VMEM] * (sum(counts) + 5),
        out_specs=[VMEM] * (n + 3),
        out_shape=[jax.ShapeDtypeStruct((halves * rows, units), BF16)] * 2
        + [TOKEN]
        + [jax.ShapeDtypeStruct((rows, width), BF16)] * n,
        compiler_params=pltpu.CompilerParams(vmem_limit_bytes=10 << 20),
        cost_estimate=pl.CostEstimate(
            flops=6 * halves * rows * parts * width * units, bytes_accessed=12 << 20, transcendentals=halves * rows * units
        ),
        name="backward",
    )(me, *[piece for chunk in g for piece in chunk], pre_gate, pre_up, w_gate, w_up, w_down)
    return out[0], out[1], out[2], [out[3 + i * halves : 3 + (i + 1) * halves] for i in range(parts)]


def weights_kernel(parts, counts, me, *refs):
    n = sum(counts)
    sources = refs[: 2 * n + 3]
    grad_gate, grad_up, grad_down, done = refs[2 * n + 4 : 2 * n + 8]
    x, g, units_in, tall, wide, in_sems, out_sems = refs[2 * n + 8 :]
    rows, width = x.shape[1:]
    done[...] = jnp.zeros(done.shape, F32)

    def fetch(kind, shift):
        first = kind * n + sum(counts[:shift])
        size = rows // counts[shift]
        return [
            pltpu.make_async_copy(
                sources[first + i], (x, g)[kind].at[shift, pl.ds(i * size, size), :], in_sems.at[first + i]
            )
            for i in range(counts[shift])
        ]

    units = [
        pltpu.make_async_copy(sources[2 * n + i], units_in.at[i], in_sems.at[2 * n + i]) for i in range(3)
    ]
    stages = [[units[1]] + fetch(0, 0), [units[2]]]
    stages += [fetch(0, shift) for shift in range(1, parts)]
    stages += [[units[0]] + fetch(1, 0)] + [fetch(1, shift) for shift in range(1, parts)]
    for stage in stages:
        for copy in stage:
            copy.start()

    def arrived(stage):
        for copy in stages[stage]:
            copy.wait()

    copies = []

    def send(kind, shift, slot, target):
        copy = pltpu.make_async_copy(slot, target, out_sems.at[kind * parts + shift])
        copy.start()
        copies.append(copy)

    for shift in range(parts):
        where = pl.ds(column_block(me, shift, parts, width), width)
        arrived(0 if shift == 0 else 1 + shift)
        tall[shift] = dot(x[shift], units_in[1], TN)
        send(0, shift, tall.at[shift], grad_gate.at[0, where, :])
        if shift == 0:
            arrived(1)
        tall[parts + shift] = dot(x[shift], units_in[2], TN)
        send(1, shift, tall.at[parts + shift], grad_up.at[0, where, :])
    for shift in range(parts):
        where = pl.ds(column_block(me, shift, parts, width), width)
        arrived(1 + parts + shift)
        wide[shift] = dot(units_in[0], g[shift], TN)
        send(2, shift, wide.at[shift], grad_down.at[0, :, where])
    for copy in copies:
        copy.wait()


def weight_grads(me, x, g, hidden, d_gate, d_up, after):
    parts, counts = len(x), tuple(map(len, x))
    rows, width = x[0][0].shape[0] * counts[0], x[0][0].shape[1]
    units = hidden.shape[1]
    n = sum(counts)
    return pl.pallas_call(
        functools.partial(weights_kernel, parts, counts),
        in_specs=[SMEM] + [HBM] * (2 * n + 3) + [VMEM],
        out_specs=[HBM] * 3 + [VMEM],
        out_shape=(
            jax.ShapeDtypeStruct((1, parts * width, units), F32),
            jax.ShapeDtypeStruct((1, parts * width, units), F32),
            jax.ShapeDtypeStruct((1, units, parts * width), F32),
            TOKEN,
        ),
        scratch_shapes=[
            pltpu.VMEM((parts, rows, width), BF16),
            pltpu.VMEM((parts, rows, width), BF16),
            pltpu.VMEM((3, rows, units), BF16),
            pltpu.VMEM((2 * parts, width, units), F32),
            pltpu.VMEM((parts, units, width), F32),
            pltpu.SemaphoreType.DMA((2 * n + 3,)),
            pltpu.SemaphoreType.DMA((3 * parts,)),
        ],
        compiler_params=pltpu.CompilerParams(vmem_limit_bytes=58 << 20),
        cost_estimate=pl.CostEstimate(
            flops=6 * rows * parts * width * units, bytes_accessed=13 << 20, transcendentals=0
        ),
        name="weight_grads",
    )(me, *[v for c in x for v in c], *[v for c in g for v in c], hidden, d_gate, d_up, after)


def total_kernel(halves, *refs):
    out, done = refs[-2:]
    terms = len(refs[:-3]) // halves
    done[...] = jnp.zeros(done.shape, F32)
    rows = refs[0].shape[0]
    step = 32

    @pl.loop(0, rows // step)
    def _(i):
        here = pl.ds(pl.multiple_of(i * step, step), step)
        for h in range(halves):
            total = refs[h * terms][here, :].astype(F32)
            for k in range(1, terms):
                total = total + refs[h * terms + k][here, :].astype(F32)
            out[pl.ds(pl.multiple_of(h * rows + i * step, step), step), :] = total.astype(BF16)


def totals(groups, after):
    rows, width = groups[0][0].shape
    return pl.pallas_call(
        functools.partial(total_kernel, len(groups)),
        in_specs=[VMEM] * sum(map(len, groups)) + [VMEM],
        out_specs=[VMEM] * 2,
        out_shape=(jax.ShapeDtypeStruct((len(groups) * rows, width), BF16), TOKEN),
        compiler_params=pltpu.CompilerParams(vmem_limit_bytes=2 << 20),
        name="totals",
    )(*[v for group in groups for v in group], after)


def assemble_kernel(parts, me, *refs):
    out, done, sems = refs[parts:]
    done[...] = jnp.zeros(done.shape, F32)
    width = refs[0].shape[1]
    copies = []
    for shift in range(parts):
        columns = pl.ds(column_block(me, shift, parts, width), width)
        copies.append(pltpu.make_async_copy(refs[shift], out.at[:, columns], sems.at[shift]))
        copies[-1].start()
    for copy in copies:
        copy.wait()


def assemble(me, chunks):
    rows, width = chunks[0].shape
    parts = len(chunks)
    return pl.pallas_call(
        functools.partial(assemble_kernel, parts),
        in_specs=[SMEM] + [VMEM] * parts,
        out_specs=[HBM, VMEM],
        out_shape=(jax.ShapeDtypeStruct((rows, width * parts), BF16), TOKEN),
        scratch_shapes=[pltpu.SemaphoreType.DMA((parts,))],
        compiler_params=pltpu.CompilerParams(vmem_limit_bytes=2 << 20),
        name="assemble",
    )(me, *chunks)


def combine_kernel(weighted, info, back, *refs):
    out = refs[-1]
    values = back[...]
    columns = info[...]
    lanes = lax.broadcasted_iota(jnp.int32, (columns.shape[0], values.shape[0]), 1)
    picked = []
    for k in range(2):
        hot = (lanes == columns[:, k : k + 1].astype(jnp.int32)).astype(F32).astype(BF16)
        row = dot(hot, values, NN)
        picked.append(row * columns[:, 2 + k : 3 + k] if weighted else row)
    out[...] = (picked[0] + picked[1]).astype(BF16)


def combine(info, back, weighted, after):
    return pl.pallas_call(
        functools.partial(combine_kernel, weighted),
        in_specs=[VMEM] * (2 + len(after)),
        out_specs=VMEM,
        out_shape=jax.ShapeDtypeStruct((info.shape[0], back.shape[1]), BF16),
        compiler_params=pltpu.CompilerParams(vmem_limit_bytes=8 << 20),
        name="combine",
    )(info, back, *after)


def swap_blocks(values):
    return lax.all_to_all(values, "expert", split_axis=0, concat_axis=0, tiled=True)


def send_back(values, experts, capacity):
    rows, width = values.shape
    return swap_blocks(values.reshape(experts, capacity, width)).reshape(rows, width)


def shift_by(values, step):
    size = lax.axis_size("tensor")
    return lax.ppermute(values, "tensor", [(i, (i + step) % size) for i in range(size)])


def gather_ring(own):
    rows = own.shape[0] // 2
    left = shift_by(own, 1)
    right = shift_by(own, -1)
    far_top = shift_by(left[:rows], 1)
    far_bottom = shift_by(right[rows:], -1)
    return [(own,), (left,), (far_top, far_bottom), (right,)]


def add(a, b):
    return (a.astype(F32) + b.astype(F32)).astype(BF16)


def scatter_ring(chunks):
    own, right, far, left = chunks
    far_top = shift_by(far[0], -1)
    far_bottom = shift_by(far[1], 1)
    from_left_top = shift_by(right[0], 1)
    from_right_bottom = shift_by(left[1], -1)
    from_right_top = shift_by(add(left[0], far_top), -1)
    from_left_bottom = shift_by(add(right[1], far_bottom), 1)
    return [
        (own[0], from_left_top, from_right_top),
        (own[1], from_right_bottom, from_left_bottom),
    ]


def gather_columns(me, values):
    far = shift_by(values, 2)
    left = shift_by(values, 1)
    right = shift_by(values, -1)
    return assemble(me, [values, left, far, right])


def shards(tokens, routes, mix_weights, w_gate, w_up, w_down, cotangent):
    experts = lax.axis_size("expert")
    parts = lax.axis_size("tensor")
    capacity = 4 * tokens.shape[0] // experts
    me = lax.axis_index("tensor").astype(jnp.int32).reshape(1)
    sent, info = dispatch(me, routes, mix_weights, tokens, cotangent, experts, capacity, parts)
    received = swap_blocks(sent)
    x = gather_ring(pick(received, 0, capacity, info))
    g = gather_ring(pick(received, capacity, capacity, info))
    pre_gate, pre_up, hidden, partial_out = forward(me, x, w_gate, w_up, w_down)
    out_terms = scatter_ring(partial_out)
    d_gate, d_up, after_backward, partial_in = backward(me, g, pre_gate, pre_up, w_gate, w_up, w_down)
    out_mine, _ = totals(out_terms, after_backward)
    out_back = send_back(out_mine, experts, capacity)
    in_mine, after_sums = totals(scatter_ring(partial_in), after_backward)
    in_back = send_back(in_mine, experts, capacity)
    grad_gate, grad_up, grad_down, after_weights = weight_grads(me, x, g, hidden, d_gate, d_up, after_sums)
    result, after_result = gather_columns(me, combine(info, out_back, True, [after_sums]))
    grad_tokens, _ = gather_columns(me, combine(info, in_back, False, [after_weights, after_result]))
    return (result, grad_tokens, grad_gate, grad_up, grad_down)


def solution(mesh):
    in_specs = (
        P("expert", None),
        P("expert", None),
        P("expert", None),
        P("expert", None, "tensor"),
        P("expert", None, "tensor"),
        P("expert", "tensor", None),
        P("expert", None),
    )
    out_specs = (
        P("expert", None),
        P("expert", None),
        P("expert", None, "tensor"),
        P("expert", None, "tensor"),
        P("expert", "tensor", None),
    )
    return jax.shard_map(shards, mesh=mesh, in_specs=in_specs, out_specs=out_specs, check_vma=False)
```

```python
import functools

import jax
import jax.numpy as jnp
from jax import lax
from jax.experimental import pallas as pl
from jax.experimental.pallas import tpu as pltpu
from jax.sharding import PartitionSpec as P

F32 = jnp.float32
BF16 = jnp.bfloat16
NN = (((1,), (0,)), ((), ()))
NT = (((1,), (1,)), ((), ()))
TN = (((0,), (0,)), ((), ()))


def dot(a, b, dims):
    return lax.dot_general(a, b, dims, preferred_element_type=F32)


VMEM = pl.BlockSpec(memory_space=pltpu.VMEM)
SMEM = pl.BlockSpec(memory_space=pltpu.SMEM)
ANY = pl.BlockSpec(memory_space=pl.ANY)
HBM = pl.BlockSpec(memory_space=pltpu.HBM)
TOKEN = jax.ShapeDtypeStruct((8, 128), F32)
MARK = jax.ShapeDtypeStruct((1,), jnp.int32)


def one_hot(place, height):
    lines = lax.broadcasted_iota(jnp.int32, (height, place.shape[1]), 0)
    return (lines == place).astype(F32).astype(BF16)


def dispatch_kernel(capacity, experts, me, routes_in, mix_in, tokens_in, cotangent_in, x_out, g_out, info, *scratch):
    routes, mix, tokens, cotangent, sems = scratch
    rows, width = tokens.shape
    mine = pl.ds(pl.multiple_of(me[0] * width, width), width)
    fetches = [
        pltpu.make_async_copy(source, slot, sems.at[i])
        for i, (source, slot) in enumerate(
            [
                (routes_in, routes),
                (mix_in, mix),
                (tokens_in.at[:, mine], tokens),
                (cotangent_in.at[:, mine], cotangent),
            ]
        )
    ]
    for fetch in fetches:
        fetch.start()
    for fetch in fetches:
        fetch.wait()
    first, second = routes[0:1, :], routes[1:2, :]
    lines = lax.broadcasted_iota(jnp.int32, (experts, rows), 0)
    hot0 = (lines == first).astype(F32)
    hot1 = (lines == second).astype(F32)
    before = lax.broadcasted_iota(jnp.int32, (rows, rows), 0) < lax.broadcasted_iota(jnp.int32, (rows, rows), 1)
    earlier = dot((hot0 + hot1).astype(BF16), before.astype(F32).astype(BF16), NN)
    rank0 = jnp.sum(earlier * hot0, axis=0, keepdims=True)
    rank1 = jnp.sum((earlier + hot0) * hot1, axis=0, keepdims=True)
    place0 = first * capacity + rank0.astype(jnp.int32)
    place1 = second * capacity + rank1.astype(jnp.int32)
    buffer_rows = experts * capacity
    pick0, pick1 = one_hot(place0, buffer_rows), one_hot(place1, buffer_rows)
    columns = jnp.concatenate(
        [place0.astype(F32), place1.astype(F32), mix[...], jnp.zeros((4, rows), F32)], axis=0
    ).T
    info[...] = columns
    x = dot(pick0 + pick1, tokens[...], NN).astype(BF16)
    x_out[...] = x.reshape(x_out.shape)
    cot = cotangent[...].astype(F32)
    scaled0 = (columns[:, 2:3] * cot).astype(BF16)
    scaled1 = (columns[:, 3:4] * cot).astype(BF16)
    g = (dot(pick0, scaled0, NN) + dot(pick1, scaled1, NN)).astype(BF16)
    g_out[...] = g.reshape(g_out.shape)


def dispatch(me, routes, mix, tokens, cotangent, experts, capacity, parts):
    rows, width = tokens.shape[0], tokens.shape[1] // parts
    return pl.pallas_call(
        functools.partial(dispatch_kernel, capacity, experts),
        in_specs=[SMEM] + [HBM] * 4,
        out_specs=[VMEM] * 3,
        out_shape=(
            jax.ShapeDtypeStruct((experts, capacity, width), BF16),
            jax.ShapeDtypeStruct((experts, capacity, width), BF16),
            jax.ShapeDtypeStruct((rows, 8), F32),
        ),
        scratch_shapes=[
            pltpu.VMEM((2, rows), jnp.int32),
            pltpu.VMEM((2, rows), F32),
            pltpu.VMEM((rows, width), BF16),
            pltpu.VMEM((rows, width), BF16),
            pltpu.SemaphoreType.DMA((4,)),
        ],
        compiler_params=pltpu.CompilerParams(vmem_limit_bytes=60 << 20),
        name="dispatch",
    )(me, routes.T, mix.T, tokens, cotangent)


def column_block(me, shift, parts, width):
    owner = lax.rem(me[0] + (parts - shift), parts)
    return pl.multiple_of(owner * width, width)


def load_kernel(after, *refs):
    count = (len(refs) - 1) // 2
    sources, slots, sems = refs[:count], refs[count : 2 * count], refs[-1]
    copies = [pltpu.make_async_copy(source, slot, sems.at[i]) for i, (source, slot) in enumerate(zip(sources, slots))]
    for copy in copies:
        copy.start()
    for copy in copies:
        copy.wait()


def load(arrays, after):
    return pl.pallas_call(
        load_kernel,
        in_specs=[VMEM] + [HBM] * len(arrays),
        out_specs=[VMEM] * len(arrays),
        out_shape=[jax.ShapeDtypeStruct(v.shape, v.dtype) for v in arrays],
        scratch_shapes=[pltpu.SemaphoreType.DMA((len(arrays),))],
        compiler_params=pltpu.CompilerParams(vmem_limit_bytes=50 << 20),
        name="load",
    )(after, *arrays)


def by_chunk(refs, counts, halves):
    chunks, at = [], 0
    for count in counts:
        if count == 1:
            rows = refs[at].shape[0] // halves
            chunks.append([refs[at].at[pl.ds(h * rows, rows), :] for h in range(halves)])
        else:
            chunks.append(list(refs[at : at + count]))
        at += count
    return chunks


def forward_kernel(parts, halves, counts, me, *refs):
    n = sum(counts)
    x = by_chunk(refs[:n], counts, halves)
    w_gate, w_up, w_down = refs[n : n + 3]
    pre_gate, pre_up, hidden = refs[n + 3 : n + 6]
    partial_out = refs[n + 6 :]
    rows, width = partial_out[0].shape
    for h in range(halves):
        gate = up = None
        for shift in range(parts):
            block = x[shift][h][...]
            lines = pl.ds(column_block(me, shift, parts, width), width)
            g = dot(block, w_gate[0, lines, :], NN)
            u = dot(block, w_up[0, lines, :], NN)
            gate, up = (g, u) if gate is None else (gate + g, up + u)
        part = pl.ds(h * rows, rows)
        pre_gate[part, :] = gate
        pre_up[part, :] = up
        act = (gate / (1.0 + jnp.exp(-gate)) * up).astype(BF16)
        hidden[part, :] = act
        for shift in range(parts):
            columns = pl.ds(column_block(me, parts - shift, parts, width), width)
            partial_out[shift * halves + h][...] = dot(act, w_down[0, :, columns], NN).astype(BF16)


def forward(me, x, w_gate, w_up, w_down):
    parts, halves, counts = len(x), 2, tuple(map(len, x))
    rows, width = x[0][0].shape[0] * counts[0] // halves, x[0][0].shape[1]
    units = w_gate.shape[2]
    n = parts * halves
    out = pl.pallas_call(
        functools.partial(forward_kernel, parts, halves, counts),
        in_specs=[SMEM] + [VMEM] * (sum(counts) + 3),
        out_specs=[VMEM] * (n + 3),
        out_shape=[jax.ShapeDtypeStruct((halves * rows, units), F32)] * 2
        + [jax.ShapeDtypeStruct((halves * rows, units), BF16)]
        + [jax.ShapeDtypeStruct((rows, width), BF16)] * n,
        compiler_params=pltpu.CompilerParams(vmem_limit_bytes=10 << 20),
        cost_estimate=pl.CostEstimate(
            flops=6 * halves * rows * parts * width * units, bytes_accessed=12 << 20, transcendentals=halves * rows * units
        ),
        name="forward",
    )(me, *[piece for chunk in x for piece in chunk], w_gate, w_up, w_down)
    return out[0], out[1], out[2], [out[3 + i * halves : 3 + (i + 1) * halves] for i in range(parts)]


def backward_kernel(parts, halves, counts, me, *refs):
    n = sum(counts)
    g = by_chunk(refs[:n], counts, halves)
    pre_gate, pre_up, w_gate, w_up, w_down = refs[n : n + 5]
    d_gate, d_up, done = refs[n + 5 : n + 8]
    partial_in = refs[n + 8 :]
    done[...] = jnp.zeros(done.shape, F32)
    rows, width = partial_in[0].shape
    for h in range(halves):
        d_hidden = None
        for shift in range(parts):
            columns = pl.ds(column_block(me, shift, parts, width), width)
            part = dot(g[shift][h][...], w_down[0, :, columns], NT)
            d_hidden = part if d_hidden is None else d_hidden + part
        mine = pl.ds(h * rows, rows)
        gate, up = pre_gate[mine, :], pre_up[mine, :]
        sigma = 1.0 / (1.0 + jnp.exp(-gate))
        dg = (d_hidden * up * sigma * (1.0 + gate * (1.0 - sigma))).astype(BF16)
        du = (d_hidden * gate * sigma).astype(BF16)
        d_gate[mine, :] = dg
        d_up[mine, :] = du
        for shift in range(parts):
            lines = pl.ds(column_block(me, parts - shift, parts, width), width)
            partial_in[shift * halves + h][...] = (
                dot(dg, w_gate[0, lines, :], NT) + dot(du, w_up[0, lines, :], NT)
            ).astype(BF16)


def backward(me, g, pre_gate, pre_up, w_gate, w_up, w_down):
    parts, halves, counts = len(g), 2, tuple(map(len, g))
    rows, width = g[0][0].shape[0] * counts[0] // halves, g[0][0].shape[1]
    units = w_gate.shape[2]
    n = parts * halves
    out = pl.pallas_call(
        functools.partial(backward_kernel, parts, halves, counts),
        in_specs=[SMEM] + [VMEM] * (sum(counts) + 5),
        out_specs=[VMEM] * (n + 3),
        out_shape=[jax.ShapeDtypeStruct((halves * rows, units), BF16)] * 2
        + [TOKEN]
        + [jax.ShapeDtypeStruct((rows, width), BF16)] * n,
        compiler_params=pltpu.CompilerParams(vmem_limit_bytes=10 << 20),
        cost_estimate=pl.CostEstimate(
            flops=6 * halves * rows * parts * width * units, bytes_accessed=12 << 20, transcendentals=halves * rows * units
        ),
        name="backward",
    )(me, *[piece for chunk in g for piece in chunk], pre_gate, pre_up, w_gate, w_up, w_down)
    return out[0], out[1], out[2], [out[3 + i * halves : 3 + (i + 1) * halves] for i in range(parts)]


def weights_kernel(parts, counts, me, *refs):
    n = sum(counts)
    sources = refs[: 2 * n + 3]
    grad_gate, grad_up, grad_down, done = refs[2 * n + 4 : 2 * n + 8]
    x, g, units_in, tall, wide, in_sems, out_sems = refs[2 * n + 8 :]
    rows, width = x.shape[1:]
    done[0] = 0

    def fetch(kind, shift):
        first = kind * n + sum(counts[:shift])
        size = rows // counts[shift]
        return [
            pltpu.make_async_copy(
                sources[first + i], (x, g)[kind].at[shift, pl.ds(i * size, size), :], in_sems.at[first + i]
            )
            for i in range(counts[shift])
        ]

    units = [
        pltpu.make_async_copy(sources[2 * n + i], units_in.at[i], in_sems.at[2 * n + i]) for i in range(3)
    ]
    stages = [[units[1]] + fetch(0, 0), [units[2]]]
    stages += [fetch(0, shift) for shift in range(1, parts)]
    stages += [[units[0]] + fetch(1, 0)] + [fetch(1, shift) for shift in range(1, parts)]
    for stage in stages:
        for copy in stage:
            copy.start()

    def arrived(stage):
        for copy in stages[stage]:
            copy.wait()

    copies = []

    def send(kind, shift, slot, target):
        copy = pltpu.make_async_copy(slot, target, out_sems.at[kind * parts + shift])
        copy.start()
        copies.append(copy)

    for shift in range(parts):
        where = pl.ds(column_block(me, shift, parts, width), width)
        arrived(0 if shift == 0 else 1 + shift)
        tall[shift] = dot(x[shift], units_in[1], TN)
        send(0, shift, tall.at[shift], grad_gate.at[0, where, :])
        if shift == 0:
            arrived(1)
        tall[parts + shift] = dot(x[shift], units_in[2], TN)
        send(1, shift, tall.at[parts + shift], grad_up.at[0, where, :])
    for shift in range(parts):
        where = pl.ds(column_block(me, shift, parts, width), width)
        arrived(1 + parts + shift)
        wide[shift] = dot(units_in[0], g[shift], TN)
        send(2, shift, wide.at[shift], grad_down.at[0, :, where])
    for copy in copies:
        copy.wait()


def weight_grads(me, x, g, hidden, d_gate, d_up, after):
    parts, counts = len(x), tuple(map(len, x))
    rows, width = x[0][0].shape[0] * counts[0], x[0][0].shape[1]
    units = hidden.shape[1]
    n = sum(counts)
    return pl.pallas_call(
        functools.partial(weights_kernel, parts, counts),
        in_specs=[SMEM] + [HBM] * (2 * n + 3) + [VMEM],
        out_specs=[HBM] * 3 + [SMEM],
        out_shape=(
            jax.ShapeDtypeStruct((1, parts * width, units), F32),
            jax.ShapeDtypeStruct((1, parts * width, units), F32),
            jax.ShapeDtypeStruct((1, units, parts * width), F32),
            MARK,
        ),
        scratch_shapes=[
            pltpu.VMEM((parts, rows, width), BF16),
            pltpu.VMEM((parts, rows, width), BF16),
            pltpu.VMEM((3, rows, units), BF16),
            pltpu.VMEM((2 * parts, width, units), F32),
            pltpu.VMEM((parts, units, width), F32),
            pltpu.SemaphoreType.DMA((2 * n + 3,)),
            pltpu.SemaphoreType.DMA((3 * parts,)),
        ],
        compiler_params=pltpu.CompilerParams(vmem_limit_bytes=58 << 20),
        cost_estimate=pl.CostEstimate(
            flops=6 * rows * parts * width * units, bytes_accessed=13 << 20, transcendentals=0
        ),
        name="weight_grads",
    )(me, *[v for c in x for v in c], *[v for c in g for v in c], hidden, d_gate, d_up, after)


def total_kernel(halves, *refs):
    out, done, mark = refs[-3:]
    terms = len(refs[:-4]) // halves
    done[...] = jnp.zeros(done.shape, F32)
    mark[0] = 0
    rows = refs[0].shape[0]
    step = 32

    @pl.loop(0, rows // step)
    def _(i):
        here = pl.ds(pl.multiple_of(i * step, step), step)
        for h in range(halves):
            total = refs[h * terms][here, :].astype(F32)
            for k in range(1, terms):
                total = total + refs[h * terms + k][here, :].astype(F32)
            out[pl.ds(pl.multiple_of(h * rows + i * step, step), step), :] = total.astype(BF16)


def totals(groups, after):
    rows, width = groups[0][0].shape
    return pl.pallas_call(
        functools.partial(total_kernel, len(groups)),
        in_specs=[VMEM] * sum(map(len, groups)) + [VMEM],
        out_specs=[VMEM] * 2 + [SMEM],
        out_shape=(jax.ShapeDtypeStruct((len(groups) * rows, width), BF16), TOKEN, MARK),
        compiler_params=pltpu.CompilerParams(vmem_limit_bytes=2 << 20),
        name="totals",
    )(*[v for group in groups for v in group], after)


def assemble_kernel(parts, me, *refs):
    out, done, sems = refs[parts:]
    done[0] = 0
    width = refs[0].shape[1]
    copies = []
    for shift in range(parts):
        columns = pl.ds(column_block(me, shift, parts, width), width)
        copies.append(pltpu.make_async_copy(refs[shift], out.at[:, columns], sems.at[shift]))
        copies[-1].start()
    for copy in copies:
        copy.wait()


def assemble(me, chunks):
    rows, width = chunks[0].shape
    parts = len(chunks)
    return pl.pallas_call(
        functools.partial(assemble_kernel, parts),
        in_specs=[SMEM] + [VMEM] * parts,
        out_specs=[HBM, SMEM],
        out_shape=(jax.ShapeDtypeStruct((rows, width * parts), BF16), MARK),
        scratch_shapes=[pltpu.SemaphoreType.DMA((parts,))],
        compiler_params=pltpu.CompilerParams(vmem_limit_bytes=2 << 20),
        name="assemble",
    )(me, *chunks)


def combine_kernel(weighted, info, back, *refs):
    out = refs[-1]
    values = back[...]
    columns = info[...]
    lanes = lax.broadcasted_iota(jnp.int32, (columns.shape[0], values.shape[0]), 1)
    picked = []
    for k in range(2):
        hot = (lanes == columns[:, k : k + 1].astype(jnp.int32)).astype(F32).astype(BF16)
        row = dot(hot, values, NN)
        picked.append(row * columns[:, 2 + k : 3 + k] if weighted else row)
    out[...] = (picked[0] + picked[1]).astype(BF16)


def combine(info, back, weighted, after):
    return pl.pallas_call(
        functools.partial(combine_kernel, weighted),
        in_specs=[VMEM] * 2 + [SMEM] * len(after),
        out_specs=VMEM,
        out_shape=jax.ShapeDtypeStruct((info.shape[0], back.shape[1]), BF16),
        compiler_params=pltpu.CompilerParams(vmem_limit_bytes=8 << 20),
        name="combine",
    )(info, back, *after)


def swap_blocks(values):
    return lax.all_to_all(values, "expert", split_axis=0, concat_axis=0, tiled=True)


def send_back(values, experts, capacity):
    rows, width = values.shape
    return swap_blocks(values.reshape(experts, capacity, width)).reshape(rows, width)


def shift_by(values, step):
    size = lax.axis_size("tensor")
    return lax.ppermute(values, "tensor", [(i, (i + step) % size) for i in range(size)])


def gather_ring(own):
    rows = own.shape[0] // 2
    left = shift_by(own, 1)
    right = shift_by(own, -1)
    far_top = shift_by(left[:rows], 1)
    far_bottom = shift_by(right[rows:], -1)
    return [(own,), (left,), (far_top, far_bottom), (right,)]


def add(a, b):
    return (a.astype(F32) + b.astype(F32)).astype(BF16)


def scatter_ring(chunks):
    own, right, far, left = chunks
    far_top = shift_by(far[0], -1)
    far_bottom = shift_by(far[1], 1)
    from_left_top = shift_by(right[0], 1)
    from_right_bottom = shift_by(left[1], -1)
    from_right_top = shift_by(add(left[0], far_top), -1)
    from_left_bottom = shift_by(add(right[1], far_bottom), 1)
    return [
        (own[0], from_left_top, from_right_top),
        (own[1], from_right_bottom, from_left_bottom),
    ]


def gather_columns(me, values):
    far = shift_by(values, 2)
    left = shift_by(values, 1)
    right = shift_by(values, -1)
    return assemble(me, [values, left, far, right])


def shards(tokens, routes, mix_weights, w_gate, w_up, w_down, cotangent):
    experts = lax.axis_size("expert")
    parts = lax.axis_size("tensor")
    capacity = 4 * tokens.shape[0] // experts
    me = lax.axis_index("tensor").astype(jnp.int32).reshape(1)
    x_sent, g_sent, info = dispatch(me, routes, mix_weights, tokens, cotangent, experts, capacity, parts)
    rows = experts * capacity
    x = gather_ring(swap_blocks(x_sent).reshape(rows, x_sent.shape[2]))
    g_mine = swap_blocks(g_sent).reshape(rows, g_sent.shape[2])
    g = gather_ring(g_mine)
    w_gate, w_up, w_down = load((w_gate, w_up, w_down), g_mine)
    pre_gate, pre_up, hidden, partial_out = forward(me, x, w_gate, w_up, w_down)
    out_terms = scatter_ring(partial_out)
    d_gate, d_up, after_backward, partial_in = backward(me, g, pre_gate, pre_up, w_gate, w_up, w_down)
    out_mine, _, _ = totals(out_terms, after_backward)
    out_back = send_back(out_mine, experts, capacity)
    in_mine, after_sums, summed = totals(scatter_ring(partial_in), after_backward)
    in_back = send_back(in_mine, experts, capacity)
    grad_gate, grad_up, grad_down, after_weights = weight_grads(me, x, g, hidden, d_gate, d_up, after_sums)
    result, after_result = gather_columns(me, combine(info, out_back, True, [summed]))
    grad_tokens, _ = gather_columns(me, combine(info, in_back, False, [after_weights, after_result]))
    return (result, grad_tokens, grad_gate, grad_up, grad_down)


def solution(mesh):
    in_specs = (
        P("expert", None),
        P("expert", None),
        P("expert", None),
        P("expert", None, "tensor"),
        P("expert", None, "tensor"),
        P("expert", "tensor", None),
        P("expert", None),
    )
    out_specs = (
        P("expert", None),
        P("expert", None),
        P("expert", None, "tensor"),
        P("expert", None, "tensor"),
        P("expert", "tensor", None),
    )
    return jax.shard_map(shards, mesh=mesh, in_specs=in_specs, out_specs=out_specs, check_vma=False)
```
